512 devices in a mesh: dp: 64 (over z, x, core), tensor: 8 (over y).
Axes of the slice: x: 4, y: 8, z: 8, core: 2. Of those that a mesh axis runs over, the one named last changes fastest.
Arguments:
- activations: bfloat16 [64, 2048, 320], P('dp'), may hold values from -6 to 6
- cotangent: bfloat16 [64, 128, 13824], P('dp', None, 'tensor'), may hold values from -3 to 3
- weight: bfloat16 [5120, 13824], P('dp', 'tensor'), may hold values from -0.078125 to 0.078125
- error_buffer: bfloat16 [64, 320, 13824], P('dp', None, 'tensor'), may hold values from -32 to 32
- warm_factor: float32 [13824, 32], P('tensor'), may hold values from -6 to 6
Outputs:
- input_gradient: bfloat16 [64, 2048, 320], P('dp', 'tensor')
- error_next: bfloat16 [64, 320, 13824], P('dp', None, 'tensor')
- update: bfloat16 [5120, 13824], P('dp', 'tensor')
The draws below stay inside these ranges and needn't reach their ends.
All inputs are finite; a program needn't handle non-finite values.
Results may differ from the reference program's by a relative error of at most 0.0012.
Values may be sent and summed in bfloat16 or wider, within the bound.
A program may use at most 64 MiB of HBM per device.

```python
import jax
import jax.numpy as jnp
from jax import lax

D = 5120
FF = 13824
RANK = 32
GROUP = 16
TOKR = 2048
REPL = 4
DSH = 320
TOKG = 128
FFW = 1728
N_DP = 64
N_TENSOR = 8


def levels(stream_key, shape, shards, smallest, largest):
    def one(axis_at, shards_of):
        heights = jax.random.uniform(jax.random.fold_in(jax.random.fold_in(stream_key, 6), axis_at), (shards_of,), jnp.float32, smallest / len(shards), largest / len(shards))
        return jnp.repeat(jnp.exp(heights), shape[axis_at] // shards_of).reshape((-1,) + (1,) * (len(shape) - axis_at - 1))

    loudness = one(*shards[0])
    for cut in shards[1:]:
        loudness = loudness * one(*cut)
    return loudness


def bell_draw(stream_key, extent, spread, bound, pieces=(), kind=jnp.bfloat16):
    values = jax.random.normal(stream_key, extent, jnp.float32) * spread
    if len(pieces) > 0:
        values = levels(stream_key, extent, pieces, -0.22, 0.18) * values
    return jnp.clip(values, min=-bound, max=bound).astype(kind)


def setup_inputs(seed: int = 0) -> dict:
    key_list = jax.random.split(jax.random.key(seed), 6)
    return {
        "activations": bell_draw(key_list[0], (N_DP, TOKR, DSH), 1.0, 6.0, ((0, 64),)),
        "cotangent": bell_draw(key_list[1], (N_DP, TOKG, FF), 0.2, 3.0, ((0, 64), (2, 8))),
        "weight": bell_draw(key_list[2], (D, FF), D ** -0.5, 0.078125, ((0, 64), (1, 8))),
        "error_buffer": bell_draw(key_list[3], (N_DP, DSH, FF), 6.0, 32.0, ((0, 64), (2, 8))),
        "warm_factor": bell_draw(key_list[4], (FF, RANK), 1.0, 6.0, ((0, 8),), jnp.float32),
    }


HIGHEST_PRECISION = lax.Precision.HIGHEST

def orthonormal(factor):
    gram_matrix = jnp.dot(factor.T, factor, precision=HIGHEST_PRECISION)
    triangle = jnp.linalg.cholesky(gram_matrix)
    return jax.scipy.linalg.solve_triangular(triangle, factor.T, lower=True).T

def reference(activations, cotangent, weight, error_buffer, warm_factor):
    tokens = activations.reshape(GROUP, REPL, TOKR, DSH).transpose(1, 2, 0, 3).reshape(REPL, TOKR, D)
    upstream = cotangent.reshape(GROUP, REPL, TOKG, FF).transpose(1, 0, 2, 3).reshape(REPL, TOKR, FF)
    carried = error_buffer.reshape(GROUP, REPL, DSH, FF).transpose(1, 0, 2, 3).reshape(REPL, D, FF)
    warm_blocks = warm_factor.reshape(N_TENSOR, FFW, RANK)
    input_parts = []
    merged = []
    factor_sum = jnp.zeros((N_TENSOR, D, RANK), jnp.float32)
    for replica in range(REPL):
        input_parts.append(jnp.dot(upstream[replica].astype(jnp.float32), weight.T.astype(jnp.float32), preferred_element_type=jnp.float32).astype(jnp.bfloat16))
        gradient = lax.dot_general(tokens[replica].astype(jnp.float32), upstream[replica].astype(jnp.float32), (((0,), (0,)), ((), ())), preferred_element_type=jnp.float32)
        merged_now = carried[replica].astype(jnp.float32) + gradient
        merged.append(merged_now)
        blocks = merged_now.reshape(D, N_TENSOR, FFW)
        factor_sum = factor_sum + jnp.einsum('dtf,tfk->tdk', blocks, warm_blocks, precision=HIGHEST_PRECISION)
    basis_blocks = jax.vmap(orthonormal)(factor_sum)
    second_factor = jnp.zeros((N_TENSOR, FFW, RANK), jnp.float32)
    for replica in range(REPL):
        blocks = merged[replica].reshape(D, N_TENSOR, FFW)
        second_factor = second_factor + jnp.einsum('dtf,tdk->tfk', blocks, basis_blocks, precision=HIGHEST_PRECISION)
    second_factor = second_factor / REPL
    approximation = jnp.einsum('tdk,tfk->dtf', basis_blocks, second_factor, precision=HIGHEST_PRECISION).reshape(D, FF)
    update = approximation.astype(jnp.bfloat16)
    error_next = jnp.stack([(merged_now - approximation).astype(jnp.bfloat16) for merged_now in merged])
    error_next = error_next.reshape(REPL, GROUP, DSH, FF).transpose(1, 0, 2, 3).reshape(N_DP, DSH, FF)
    input_gradient = jnp.stack(input_parts).reshape(REPL, TOKR, GROUP, DSH).transpose(2, 0, 1, 3).reshape(N_DP, TOKR, DSH)
    return (input_gradient, error_next, update)
```

```python
import jax
import jax.numpy as jnp
from jax import lax
from jax.experimental import pallas as pl
from jax.experimental.pallas import tpu as pltpu
from jax.sharding import PartitionSpec as P

F32 = jnp.float32
BF16 = jnp.bfloat16
MESH = pl.DeviceIdType.MESH
NZ = 8
NO = 8
NY = 8
TOK = 128
HIDDEN = 1728
WIDTH = 320
RANK = 32
ROWS = 80
NN = (((1,), (0,)), ((), ()))
NT = (((1,), (1,)), ((), ()))
TN = (((0,), (0,)), ((), ()))


def dot(a, b, dims):
    return lax.dot_general(a, b, dims, preferred_element_type=F32)


def split3(value):
    high = value.astype(BF16)
    rest = value - high.astype(F32)
    middle = rest.astype(BF16)
    low = (rest - middle.astype(F32)).astype(BF16)
    return high, middle, low


def dot_rows(value, exact, dims):
    rows = value.shape[0]
    out = dot(jnp.concatenate(split3(value), axis=0), exact, dims)
    return out[:rows] + out[rows : 2 * rows] + out[2 * rows :]


def dot_full(a, b, dims):
    return lax.dot_general(a, b, dims, precision=lax.Precision.HIGHEST, preferred_element_type=F32)


def kernel(
    x_hbm, g_hbm, w_hbm, e_hbm, f_hbm,
    dx_out, err_out, upd_out,
    gbuf, xv, wslab, ev, fv, macc, abuf,
    part, rx, rxb,
    tbuf, pbuf, ybuf, yin, gram_own, gram_in, ymsg, yall,
    sbuf, sin, s2, s2in, s3, s4, gfull,
    lsem, gx_s, gx_r, gz_s, gz_r, w_s, w_r, t_s, t_r, tx_s, tx_r, p_s, p_r,
    yx_s, yx_r, yz_s, yz_r, s1_s, s1_r, s2_s, s2_r, s3_s, s3_r, s4_s, s4_r,
    dx_s, dx_r, dxb_r,
):
    me = lax.axis_index("dp")
    y = lax.axis_index("tensor")
    z = me // NO
    slot = me % NO
    rep = me % 4
    xh = slot // 4
    own = 2 * z + xh

    def at_z(j):
        return {"dp": ((z + j + NZ) % NZ) * NO + slot, "tensor": y}

    def at_slot(j):
        return {"dp": me - slot + (slot + j) % NO, "tensor": y}

    def at_rep(j):
        return {"dp": me - rep + (rep + j) % 4, "tensor": y}

    partner = {"dp": me + 4 - 8 * xh, "tensor": y}

    def at_y(j):
        return {"dp": me, "tensor": (y + j + NY) % NY}

    def remote(src, dst, send, recv, device):
        return pltpu.make_async_remote_copy(
            src_ref=src, dst_ref=dst, send_sem=send, recv_sem=recv,
            device_id=device, device_id_type=MESH,
        )

    sent = []

    def send(*args):
        copy = remote(*args)
        copy.start()
        sent.append(copy)
        return copy

    my_rows = pl.ds(pl.multiple_of(rep * ROWS, 16), ROWS)
    local = [
        pltpu.make_async_copy(g_hbm.at[0], gbuf.at[own], lsem.at[0]),
        pltpu.make_async_copy(f_hbm, fv, lsem.at[1]),
        pltpu.make_async_copy(e_hbm.at[0], ev, lsem.at[2]),
        pltpu.make_async_copy(x_hbm.at[0], xv, lsem.at[3]),
        pltpu.make_async_copy(w_hbm, wslab.at[my_rows], lsem.at[4]),
    ]
    for copy in local:
        copy.start()

    barrier = pltpu.get_barrier_semaphore()
    greet = [at_z(j) for j in range(1, NZ)] + [at_slot(j) for j in range(1, NO)] + [at_y(1), at_y(-1)]
    for device in greet:
        pl.semaphore_signal(barrier, inc=1, device_id=device, device_id_type=MESH)
    pl.semaphore_wait(barrier, len(greet))

    def chunk_of(shift, other):
        return 2 * ((z + shift + NZ) % NZ) + (1 - xh if other else xh)

    def ring(direction, hop, other):
        sign = 1 if direction == 0 else -1
        chunk = chunk_of(-sign * (hop - 1), other)
        k = direction * 8 + (hop - 1) * 2 + other
        return remote(gbuf.at[chunk], gbuf.at[chunk], gz_s.at[k], gz_r.at[k], at_z(sign))

    def ring_send(direction, hop, other):
        copy = ring(direction, hop, other)
        copy.start()
        sent.append(copy)

    def ring_wait(direction, hop, other):
        ring(direction, hop, other).wait_recv()

    local[0].wait()
    ring_send(0, 1, 0)
    ring_send(1, 1, 0)
    swap = send(gbuf.at[own], gbuf.at[own], gx_s.at[0], gx_r.at[0], partner)

    local[1].wait()
    factor = fv[...].T
    factor3 = jnp.concatenate(split3(factor), axis=0)

    def add3(v):
        return v[:RANK] + v[RANK : 2 * RANK] + v[2 * RANK :]

    tbuf[z, xh] = add3(dot(factor3, gbuf[own], NT))
    tz = [send(tbuf.at[z, xh], tbuf.at[z, xh], t_s.at[j - 1], t_r.at[j - 1], at_z(j)) for j in range(1, NZ)]
    local[4].wait()
    wcopies = [
        send(wslab.at[my_rows], wslab.at[my_rows], w_s.at[j - 1], w_r.at[j - 1], at_rep(j)) for j in range(1, 4)
    ]
    local[2].wait()
    local[3].wait()
    macc[...] = ev[...].astype(F32)
    p_part = add3(dot(factor3, ev[...], NT))

    pending = []

    def dx_hop(chunk, stage):
        root = chunk // 2
        d = (root - y + NY) % NY
        up = remote(part.at[chunk], rx.at[chunk], dx_s.at[chunk], dx_r.at[chunk], at_y(1))
        down = remote(part.at[chunk], rx.at[chunk], dx_s.at[chunk], dx_r.at[chunk], at_y(-1))
        down_root = remote(part.at[chunk], rxb.at[chunk % 2], dx_s.at[chunk], dxb_r.at[chunk % 2], at_y(-1))
        if stage == 0:

            @pl.when(d == 4)
            def _():
                up.start()

            @pl.when(d == 5)
            def _():
                down.start()

        elif stage < 4:
            up_d = 4 - stage
            down_d = 5 + stage

            @pl.when(d == up_d)
            def _():
                up.wait_recv()
                part[chunk] += rx[chunk]
                up.start()

            if down_d < NY:

                @pl.when(d == down_d)
                def _():
                    down.wait_recv()
                    part[chunk] += rx[chunk]
                    if down_d == NY - 1:
                        down_root.start()
                    else:
                        down.start()

        else:

            @pl.when(d == 0)
            def _():
                up.wait_recv()
                down_root.wait_recv()
                total = part[chunk] + rx[chunk] + rxb[chunk % 2]
                row = pl.multiple_of((chunk % 2) * TOK, TOK)
                dx_out[0, pl.ds(row, TOK), :] = total.astype(BF16)

    def advance():
        for entry in pending:
            if entry[1] <= 4:
                dx_hop(entry[0], entry[1])
                entry[1] += 1

    def accumulate(chunk):
        tokens = xv[pl.ds(pl.multiple_of(chunk * TOK, TOK), TOK), :]
        for start in range(0, HIDDEN, 512):
            stop = min(start + 512, HIDDEN)
            macc[:, start:stop] += dot(tokens, gbuf[chunk, :, start:stop], TN)

    def input_part(chunk):
        part[chunk] = dot(gbuf[chunk], wslab[...], NT)
        dx_hop(chunk, 0)
        pending.append([chunk, 1])

    def process(chunk):
        accumulate(chunk)
        input_part(chunk)

    accumulate(own)

    for copy in tz:
        copy.wait_recv()
    tx = send(tbuf.at[:, xh], tbuf.at[:, xh], tx_s.at[0], tx_r.at[0], partner)
    tx.wait_recv()
    t_all = jnp.concatenate([tbuf[i // 2, i % 2] for i in range(2 * NZ)], axis=1)
    pbuf[rep] = p_part + dot_rows(t_all, xv[...], NN)
    pcopies = [send(pbuf.at[rep], pbuf.at[rep], p_s.at[j - 1], p_r.at[j - 1], at_rep(j)) for j in range(1, 4)]

    swap.wait_recv()
    ring_send(0, 1, 1)
    ring_send(1, 1, 1)
    for copy in wcopies:
        copy.wait_recv()
    input_part(own)
    process(chunk_of(0, 1))

    for copy in pcopies:
        copy.wait_recv()
    p_t = pbuf[0] + pbuf[1] + pbuf[2] + pbuf[3]
    gram = dot_full(p_t, p_t, NT)
    for i in range(4):
        gram_own[:, RANK * i : RANK * (i + 1)] = gram[8 * i : 8 * (i + 1), :]
    y_t = dot_rows(p_t, xv[...], NT)
    for i in range(2 * NZ):
        ybuf[i % 2, i // 2] = y_t[:, TOK * i : TOK * (i + 1)]
    yx = [
        send(ybuf.at[1 - xh], yin, yx_s.at[0], yx_r.at[0], partner),
        send(gram_own, gram_in, yx_s.at[1], yx_r.at[1], partner),
    ]

    def ring_group(hop, other):
        last = NZ // 2
        new = []
        for direction in range(2):
            if hop == last and direction != other:
                continue
            ring_wait(direction, hop, other)
            if hop + 1 < last or (hop + 1 == last and direction == other):
                ring_send(direction, hop + 1, other)
            new.append(chunk_of(-hop if direction == 0 else hop, other))
        advance()
        for chunk in new:
            process(chunk)

    ring_group(1, 0)

    for copy in yx:
        copy.wait_recv()
    pair_gram = gram_own[...] + gram_in[...]
    for i in range(NZ):
        ymsg[i, :RANK] = ybuf[xh, i] + yin[i]
        ymsg[i, RANK:] = pair_gram
    yall[z] = ymsg[z]
    yz = [
        send(ymsg.at[(z + j) % NZ], yall.at[z], yz_s.at[j - 1], yz_r.at[j - 1], at_z(j)) for j in range(1, NZ)
    ]

    ring_group(1, 1)

    for copy in yz:
        copy.wait_recv()
    y_sum = yall[0]
    for i in range(1, NZ):
        y_sum = y_sum + yall[i]
    s_t = dot_rows(p_t, ev[...], NN) + dot_rows(y_sum[:RANK], gbuf[own], NN)
    sbuf[6] = jnp.zeros_like(sbuf[6])
    sbuf[7] = jnp.zeros_like(sbuf[7])
    for i in range(7):
        width = min(256, HIDDEN - 256 * i)
        sbuf[i, :, :width] = s_t[:, 256 * i : 256 * i + width]
    sin[slot] = sbuf[slot]
    s1 = [
        send(sbuf.at[(slot + j) % NO], sin.at[slot], s1_s.at[j - 1], s1_r.at[j - 1], at_slot(j))
        for j in range(1, NO)
    ]

    for i in range(4):
        gfull[8 * i : 8 * (i + 1), :RANK] = y_sum[RANK:, RANK * i : RANK * (i + 1)]
    row_id = lax.broadcasted_iota(jnp.int32, (RANK, 128), 0)
    lane_id = lax.broadcasted_iota(jnp.int32, (RANK, 128), 1)
    work = jnp.where(lane_id < RANK, gfull[...], jnp.where(lane_id == row_id + RANK, 1.0, 0.0))
    for j in range(RANK):
        ratio = work[:, j : j + 1] / work[j : j + 1, j : j + 1]
        ratio = jnp.where(row_id[:, :1] > j, ratio, 0.0)
        work = work - ratio * work[j : j + 1, :]
    pivots = jnp.sum(jnp.where(lane_id == row_id, work, 0.0), axis=1, keepdims=True)
    inverse = (work / jnp.sqrt(pivots))[:, RANK : 2 * RANK]
    basis = dot_full(inverse, p_t, NN)

    ring_group(2, 0)

    for copy in s1:
        copy.wait_recv()
    total = sin[0]
    for i in range(1, NO):
        total = total + sin[i]
    for i in range(NZ):
        s2[i] = total[8 * (i // 2) : 8 * (i // 2) + 8, 128 * (i % 2) : 128 * (i % 2) + 128]
    s2in[z] = s2[z]
    s2c = [
        send(s2.at[(z + j) % NZ], s2in.at[z], s2_s.at[j - 1], s2_r.at[j - 1], at_z(j)) for j in range(1, NZ)
    ]

    ring_group(2, 1)

    for copy in s2c:
        copy.wait_recv()
    tile = s2in[0]
    for i in range(1, NZ):
        tile = tile + s2in[i]
    s3[z] = tile
    s3c = [send(s3.at[z], s3.at[z], s3_s.at[j - 1], s3_r.at[j - 1], at_z(j)) for j in range(1, NZ)]

    ring_group(3, 0)

    for copy in s3c:
        copy.wait_recv()
    for i in range(NZ):
        s4[slot, 8 * (i // 2) : 8 * (i // 2) + 8, 128 * (i % 2) : 128 * (i % 2) + 128] = s3[i]
    s4c = [
        send(s4.at[slot], s4.at[slot], s4_s.at[j - 1], s4_r.at[j - 1], at_slot(j)) for j in range(1, NO)
    ]

    ring_group(3, 1)

    for copy in s4c:
        copy.wait_recv()
    s_all = jnp.concatenate([s4[i] for i in range(7)], axis=1)[:, :HIDDEN]
    second = dot_full(inverse, s_all, NN) * 0.25
    bh, bm, bl = split3(basis)
    qh, qm, ql = split3(second)
    left = jnp.concatenate([bh, bh, bm, bh, bl, bm], axis=0)
    right = jnp.concatenate([qh, qm, qh, ql, qh, qm], axis=0)
    for start in range(0, HIDDEN, 512):
        stop = min(start + 512, HIDDEN)
        block = dot(left, right[:, start:stop], TN)
        abuf[:, start:stop] = block
        macc[:, start:stop] -= block
    upd_out[...] = abuf[my_rows, :].astype(BF16)

    ring_group(4, 0)
    ring_group(4, 1)
    err_out[0] = macc[...].astype(BF16)
    for _ in range(4):
        advance()

    for copy in sent:
        copy.wait_send()
    for shift in range(NZ):
        for other in range(2):
            chunk = chunk_of(shift, other)

            @pl.when((chunk // 2 - y + NY) % NY != 0)
            def _():
                remote(
                    part.at[chunk], rx.at[chunk], dx_s.at[chunk], dx_r.at[chunk], at_y(1)
                ).wait_send()


def body(activations, cotangent, weight, error_buffer, warm_factor):
    dma = pltpu.SemaphoreType.DMA
    sems = [
        dma((5,)), dma((1,)), dma((1,)), dma((16,)), dma((16,)), dma((3,)), dma((3,)), dma((7,)), dma((7,)),
        dma((1,)), dma((1,)), dma((3,)), dma((3,)), dma((2,)), dma((2,)), dma((7,)), dma((7,)),
        dma((7,)), dma((7,)), dma((7,)), dma((7,)), dma((7,)), dma((7,)), dma((7,)), dma((7,)),
        dma((16,)), dma((16,)), dma((2,)),
    ]
    vmem = pltpu.VMEM
    scratch = [
        vmem((16, TOK, HIDDEN), BF16),
        vmem((16 * TOK, WIDTH), BF16),
        vmem((WIDTH, HIDDEN), BF16),
        vmem((WIDTH, HIDDEN), BF16),
        vmem((HIDDEN, RANK), F32),
        vmem((WIDTH, HIDDEN), F32),
        vmem((WIDTH, HIDDEN), F32),
        vmem((16, TOK, WIDTH), F32),
        vmem((16, TOK, WIDTH), F32),
        vmem((2, TOK, WIDTH), F32),
        vmem((NZ, 2, RANK, TOK), F32),
        vmem((4, RANK, WIDTH), F32),
        vmem((2, NZ, RANK, TOK), F32),
        vmem((NZ, RANK, TOK), F32),
        vmem((8, 128), F32),
        vmem((8, 128), F32),
        vmem((NZ, RANK + 8, 128), F32),
        vmem((NZ, RANK + 8, 128), F32),
        vmem((NO, RANK, 256), F32),
        vmem((NO, RANK, 256), F32),
        vmem((NZ, 8, 128), F32),
        vmem((NZ, 8, 128), F32),
        vmem((NZ, 8, 128), F32),
        vmem((NO, RANK, 256), F32),
        vmem((RANK, 128), F32),
    ]
    anyspec = pl.BlockSpec(memory_space=pl.ANY)
    vspec = pl.BlockSpec(memory_space=pltpu.VMEM)
    return pl.pallas_call(
        kernel,
        out_shape=(
            jax.ShapeDtypeStruct((1, 2 * TOK, WIDTH), BF16),
            jax.ShapeDtypeStruct((1, WIDTH, HIDDEN), BF16),
            jax.ShapeDtypeStruct((ROWS, HIDDEN), BF16),
        ),
        in_specs=[anyspec] * 5,
        out_specs=(vspec, vspec, vspec),
        scratch_shapes=scratch + sems,
        compiler_params=pltpu.CompilerParams(
            collective_id=0, has_side_effects=True, vmem_limit_bytes=56 * 1024 * 1024
        ),
        cost_estimate=pl.CostEstimate(flops=4600000000, bytes_accessed=8000000, transcendentals=0),
    )(activations, cotangent, weight, error_buffer, warm_factor)


def solution(mesh):
    in_specs = (
        P("dp", None, None),
        P("dp", None, "tensor"),
        P("dp", "tensor"),
        P("dp", None, "tensor"),
        P("tensor", None),
    )
    out_specs = (P("dp", "tensor", None), P("dp", None, "tensor"), P("dp", "tensor"))
    return jax.shard_map(body, mesh=mesh, in_specs=in_specs, out_specs=out_specs, check_vma=False)
```

```python
import jax
import jax.numpy as jnp
from jax import lax
from jax.experimental import pallas as pl
from jax.experimental.pallas import tpu as pltpu
from jax.sharding import PartitionSpec as P

F32 = jnp.float32
BF16 = jnp.bfloat16
MESH = pl.DeviceIdType.MESH
NZ = 8
NO = 8
NY = 8
TOK = 128
HIDDEN = 1728
WIDTH = 320
RANK = 32
ROWS = 80
PIECES = 6
PIECE = HIDDEN // PIECES
SUBS = 4
SPACING = 8
DEPTH = 4
SUB = WIDTH // SUBS
NN = (((1,), (0,)), ((), ()))
NT = (((1,), (1,)), ((), ()))
TN = (((0,), (0,)), ((), ()))


def dot(a, b, dims):
    return lax.dot_general(a, b, dims, preferred_element_type=F32)


def split3(value):
    high = value.astype(BF16)
    rest = value - high.astype(F32)
    middle = rest.astype(BF16)
    low = (rest - middle.astype(F32)).astype(BF16)
    return high, middle, low


def dot_rows(value, exact, dims):
    rows = value.shape[0]
    out = dot(jnp.concatenate(split3(value), axis=0), exact, dims)
    return out[:rows] + out[rows : 2 * rows] + out[2 * rows :]


def dot_full(a, b, dims):
    return lax.dot_general(a, b, dims, precision=lax.Precision.HIGHEST, preferred_element_type=F32)


def kernel(
    x_hbm, g_hbm, w_hbm, e_hbm, f_hbm,
    dx_out, err_out, upd_out,
    gbuf, xv, wslab, ev, fv, macc, abuf,
    part, rx, rxb, p_part,
    tbuf, pbuf, gram_own, ymsg, yall,
    sbuf, sin, s2, s2in, s3, s4, gfull,
    lsem, gx_s, gx_r, gz_s, gz_r, w_s, w_r, t_s, t_r, p_s, p_r,
    yz_s, yz_r, s1_s, s1_r, s2_s, s2_r, s3_s, s3_r, s4_s, s4_r,
    dx_s, dx_r, dxb_r,
):
    me = lax.axis_index("dp")
    y = lax.axis_index("tensor")
    z = me // NO
    slot = me % NO
    rep = me % 4
    xh = slot // 4
    own = 2 * z + xh

    def at_z(j):
        return {"dp": ((z + j + NZ) % NZ) * NO + slot, "tensor": y}

    def at_slot(j):
        return {"dp": me - slot + (slot + j) % NO, "tensor": y}

    def at_rep(j):
        return {"dp": me - rep + (rep + j) % 4, "tensor": y}

    partner = {"dp": me + 4 - 8 * xh, "tensor": y}

    def at_y(j):
        return {"dp": me, "tensor": (y + j + NY) % NY}

    def at_chunk(chunk):
        return {"dp": (chunk // 2) * NO + slot % 4 + 4 * (chunk % 2), "tensor": y}

    def remote(src, dst, send, recv, device):
        return pltpu.make_async_remote_copy(
            src_ref=src, dst_ref=dst, send_sem=send, recv_sem=recv,
            device_id=device, device_id_type=MESH,
        )

    sent = []

    def chain_send(*args):
        return send(*args)

    def send(*args):
        copy = remote(*args)
        copy.start()
        sent.append(copy)
        return copy

    my_rows = pl.ds(pl.multiple_of(rep * ROWS, 16), ROWS)
    local = [
        pltpu.make_async_copy(g_hbm.at[0], gbuf.at[own], lsem.at[0]),
        pltpu.make_async_copy(f_hbm, fv, lsem.at[1]),
        pltpu.make_async_copy(e_hbm.at[0], ev, lsem.at[2]),
        pltpu.make_async_copy(x_hbm.at[0], xv, lsem.at[3]),
        pltpu.make_async_copy(w_hbm, wslab.at[my_rows], lsem.at[4]),
    ]
    for copy in local:
        copy.start()

    barrier = pltpu.get_barrier_semaphore()
    greet = [at_chunk((own + j) % 16) for j in range(1, 16)] + [at_slot(j) for j in range(1, NO) if j != 4]
    greet += [at_y(j) for j in (-3, -2, -1, 1, 2, 3)]
    for device in greet:
        pl.semaphore_signal(barrier, inc=1, device_id=device, device_id_type=MESH)
    pl.semaphore_wait(barrier, len(greet))

    def chunk_of(shift, other):
        return 2 * ((z + shift + NZ) % NZ) + (1 - xh if other else xh)

    def pieces_of(direction, hop, other):
        if hop < NZ // 2:
            return range(PIECES)
        half = PIECES // 2
        return range(half) if direction == 0 else range(half, PIECES)

    def ring(direction, hop, other, piece):
        sign = 1 if direction == 0 else -1
        ref = gbuf.at[chunk_of(-sign * (hop - 1), other), pl.ds(piece * PIECE, PIECE)]
        k = ((direction * 4 + hop - 1) * 2 + other) * PIECES + piece
        return remote(ref, ref, gz_s.at[k], gz_r.at[k], at_z(sign))

    queues = [[], []]
    counts = [[0, 0], [0, 0]]

    def issue(direction):
        count = counts[direction]
        while queues[direction] and count[0] < count[1] + DEPTH:
            copy = ring(direction, *queues[direction].pop(0))
            copy.start()
            sent.append(copy)
            count[0] += 1

    def ring_send(direction, hop, other, piece):
        queues[direction].append((hop, other, piece))

    SHIFTS = (0, -3, 3, 4)

    def cross(k, piece):
        ref = gbuf.at[chunk_of(SHIFTS[k], 0), pl.ds(piece * PIECE, PIECE)]
        return remote(ref, ref, gx_s.at[k * PIECES + piece], gx_r.at[k * PIECES + piece], partner)

    def cross_send(k, piece):
        copy = cross(k, piece)
        copy.start()
        sent.append(copy)

    def cross_wait(k):
        for piece in range(PIECES):
            cross(k, piece).wait_recv()

    def arrive(hop, other, work):
        for step in range(len(pieces_of(0, hop, other))):
            for direction in range(2):
                piece = pieces_of(direction, hop, other)[step]
                ring(direction, hop, other, piece).wait_recv()
                counts[direction][1] += 1
                reach = 2 if other else 4
                if hop < reach and piece in pieces_of(direction, hop + 1, other):
                    ring_send(direction, hop + 1, other, piece)
                issue(direction)
                if not other and hop == 3:
                    cross_send(1 + direction, piece)
                if not other and hop == 4:
                    cross_send(3, piece)
            advance()
            for task in work.get(step, ()):
                task()

    local[0].wait()
    local[1].wait()

    factor3 = jnp.concatenate(split3(fv[...]), axis=0)

    def add3(v):
        return v[:RANK] + v[RANK : 2 * RANK] + v[2 * RANK :]

    tbuf[own] = add3(dot(factor3, gbuf[own], NN))
    tz = [
        chain_send(tbuf.at[own], tbuf.at[own], t_s.at[j - 1], t_r.at[j - 1], at_chunk((own + j) % 16))
        for j in range(1, 16)
    ]
    for piece in range(PIECES):
        ring_send(0, 1, 0, piece)
        ring_send(1, 1, 0, piece)
    issue(0)
    issue(1)
    local[4].wait()
    wcopies = [
        send(wslab.at[my_rows], wslab.at[my_rows], w_s.at[j - 1], w_r.at[j - 1], at_rep(j)) for j in range(1, 4)
    ]
    for piece in range(PIECES):
        cross_send(0, piece)
    local[2].wait()
    local[3].wait()
    macc[...] = ev[...].astype(F32)
    p_part[...] = add3(dot(factor3, ev[...], NT))

    pending = []

    def dx_hop(chunk, stage):
        turn = 1 - 2 * (chunk % 2)
        root = chunk // 2
        d = (turn * (root - y) + 2 * NY) % NY

        def near(sub, step):
            rows = pl.ds(sub * SUB, SUB)
            return remote(
                part.at[chunk, rows], rx.at[chunk, rows], dx_s.at[chunk], dx_r.at[chunk * SUBS + sub], at_y(step)
            )

        def last(sub, distance):
            rows = pl.ds(sub * SUB, SUB)
            k = chunk % 2 * NY + distance
            return remote(
                part.at[chunk, rows], rxb.at[k, rows], dx_s.at[chunk], dxb_r.at[k * SUBS + sub],
                {"dp": me, "tensor": root},
            )

        if stage == 0:

            @pl.when((d == 4) | (d == 2))
            def _():
                for sub in range(SUBS):
                    near(sub, turn).start()

            @pl.when(d == 5)
            def _():
                for sub in range(SUBS):
                    near(sub, -turn).start()

            @pl.when(d == 7)
            def _():
                for sub in range(SUBS):
                    last(sub, d).start()

        elif stage == 1:

            @pl.when((d == 1) | (d == 3) | (d == 6))
            def _():
                for sub in range(SUBS):
                    near(sub, turn).wait_recv()
                    rows = pl.ds(sub * SUB, SUB)
                    part[chunk, rows] += rx[chunk, rows]
                    last(sub, d).start()

        else:

            @pl.when(d == 0)
            def _():
                lane = pl.multiple_of((chunk % 2) * TOK, TOK)
                for sub in range(SUBS):
                    rows = pl.ds(sub * SUB, SUB)
                    total = part[chunk, rows]
                    for distance in (7, 1, 6, 3):
                        arrived = remote(
                            part.at[chunk, rows], rxb.at[chunk % 2 * NY + distance, rows], dx_s.at[chunk],
                            dxb_r.at[(chunk % 2 * NY + distance) * SUBS + sub], at_y(1),
                        )
                        arrived.wait_recv()
                        total += rxb[chunk % 2 * NY + distance, rows]
                    dx_out[0, rows, pl.ds(lane, TOK)] = total.astype(BF16)

    clock = [0]

    def advance(spacing=SPACING):
        clock[0] += 1
        for stage in (1,):
            for entry in pending:
                if entry[1] == stage and clock[0] - entry[2] >= spacing:
                    dx_hop(entry[0], stage)
                    entry[1:] = [stage + 1, clock[0]]

    def accumulate(chunk):
        tokens = xv[:, pl.ds(pl.multiple_of(chunk * TOK, TOK), TOK)]
        for start in range(0, HIDDEN, 512):
            stop = min(start + 512, HIDDEN)
            macc[:, start:stop] += dot(tokens, gbuf[chunk, start:stop, :], NT)

    def process(*chunks):
        for chunk in chunks:
            accumulate(chunk)
        for chunk in chunks:
            part[chunk] = dot(wslab[...], gbuf[chunk], NN)
            dx_hop(chunk, 0)
            pending.append([chunk, 1, clock[0]])

    flight = {}

    def wait_for(name):
        for copy in flight[name]:
            copy.wait_recv()

    def left_factor():
        wait_for("tz")
        t_all = jnp.concatenate([tbuf[i] for i in range(16)], axis=1)
        pbuf[rep] = p_part[...] + dot_rows(t_all, xv[...], NT)
        flight["p"] = [
            chain_send(pbuf.at[rep], pbuf.at[rep], p_s.at[j - 1], p_r.at[j - 1], at_rep(j)) for j in range(1, 4)
        ]

    def project_tokens():
        wait_for("p")
        p_t = pbuf[0] + pbuf[1] + pbuf[2] + pbuf[3]
        p_part[...] = p_t
        gram = dot_full(p_t, p_t, NT)
        for i in range(4):
            gram_own[:, RANK * i : RANK * (i + 1)] = gram[8 * i : 8 * (i + 1), :]
        packed = gram_own[...]
        y_t = dot_rows(p_t, xv[...], NN)
        for i in range(16):
            ymsg[i, :RANK] = y_t[:, TOK * i : TOK * (i + 1)]
            ymsg[i, RANK:] = packed
        yall[own] = ymsg[own]
        flight["yz"] = [
            chain_send(
                ymsg.at[(own + j) % 16], yall.at[own], yz_s.at[j - 1], yz_r.at[j - 1], at_chunk((own + j) % 16)
            )
            for j in range(1, 16)
        ]
        sbuf[6] = jnp.zeros_like(sbuf[6])
        sbuf[7] = jnp.zeros_like(sbuf[7])
        s_t = dot_rows(p_part[...], ev[...], NN)
        for i in range(7):
            width = min(256, HIDDEN - 256 * i)
            sbuf[i, :, :width] = s_t[:, 256 * i : 256 * i + width]

    def right_factor():
        wait_for("yz")
        y_sum = yall[0]
        for i in range(1, 16):
            y_sum = y_sum + yall[i]
        s_t = dot_rows(y_sum[:RANK], gbuf[own], NT)
        for i in range(7):
            width = min(256, HIDDEN - 256 * i)
            sbuf[i, :, :width] += s_t[:, 256 * i : 256 * i + width]
        sin[slot] = sbuf[slot]
        flight["s1"] = [
            chain_send(sbuf.at[(slot + j) % NO], sin.at[slot], s1_s.at[j - 1], s1_r.at[j - 1], at_slot(j))
            for j in range(1, NO)
        ]
        for i in range(4):
            gfull[8 * i : 8 * (i + 1), :RANK] = y_sum[RANK:, RANK * i : RANK * (i + 1)]

    row_id = lax.broadcasted_iota(jnp.int32, (RANK, 128), 0)
    lane_id = lax.broadcasted_iota(jnp.int32, (RANK, 128), 1)

    def eliminate(first, last):
        work = gfull[...]
        if first == 0:
            work = jnp.where(lane_id < RANK, work, jnp.where(lane_id == row_id + RANK, 1.0, 0.0))
        for j in range(first, last):
            ratio = work[:, j : j + 1] / work[j : j + 1, j : j + 1]
            ratio = jnp.where(row_id[:, :1] > j, ratio, 0.0)
            work = work - ratio * work[j : j + 1, :]
        gfull[...] = work

    def scatter_right():
        wait_for("s1")
        total = sin[0]
        for i in range(1, NO):
            total = total + sin[i]
        for i in range(NZ):
            s2[i] = total[8 * (i // 2) : 8 * (i // 2) + 8, 128 * (i % 2) : 128 * (i % 2) + 128]
        s2in[z] = s2[z]
        flight["s2"] = [
            chain_send(s2.at[(z + j) % NZ], s2in.at[z], s2_s.at[j - 1], s2_r.at[j - 1], at_z(j))
            for j in range(1, NZ)
        ]

    def gather_tile():
        wait_for("s2")
        tile = s2in[0]
        for i in range(1, NZ):
            tile = tile + s2in[i]
        s3[z] = tile
        flight["s3"] = [
            chain_send(s3.at[z], s3.at[z], s3_s.at[j - 1], s3_r.at[j - 1], at_z(j)) for j in range(1, NZ)
        ]

    def gather_right():
        wait_for("s3")
        for i in range(NZ):
            s4[slot, 8 * (i // 2) : 8 * (i // 2) + 8, 128 * (i % 2) : 128 * (i % 2) + 128] = s3[i]
        flight["s4"] = [
            chain_send(s4.at[slot], s4.at[slot], s4_s.at[j - 1], s4_r.at[j - 1], at_slot(j)) for j in range(1, NO)
        ]

    def finish_basis():
        work = gfull[...]
        pivots = jnp.sum(jnp.where(lane_id == row_id, work, 0.0), axis=1, keepdims=True)
        gfull[...] = work / jnp.sqrt(pivots)
        p_part[...] = dot_full(gfull[:, RANK : 2 * RANK], p_part[...], NN)

    def approximate():
        wait_for("s4")
        inverse = gfull[:, RANK : 2 * RANK]
        s_all = jnp.concatenate([s4[i] for i in range(7)], axis=1)[:, :HIDDEN]
        second = dot_full(inverse, s_all, NN) * 0.25
        bh, bm, bl = split3(p_part[...])
        qh, qm, ql = split3(second)
        left = jnp.concatenate([bh, bh, bm, bh, bl, bm], axis=0)
        right = jnp.concatenate([qh, qm, qh, ql, qh, qm], axis=0)
        for start in range(0, HIDDEN, 512):
            stop = min(start + 512, HIDDEN)
            block = dot(left, right[:, start:stop], TN)
            abuf[:, start:stop] = block
            macc[:, start:stop] -= block
        upd_out[...] = abuf[my_rows, :].astype(BF16)

    def some(*chunks):
        return lambda: process(*chunks)

    def weights_in():
        for copy in wcopies:
            copy.wait_recv()

    def send_partner_chunk():
        for piece in range(PIECES):
            cross(0, piece).wait_recv()
            ring_send(0, 1, 1, piece)
            ring_send(1, 1, 1, piece)
        issue(0)
        issue(1)

    flight["tz"] = tz
    arrive(1, 0, {})
    arrive(
        2,
        0,
        {
            0: [left_factor],
            1: [weights_in, some(own)],
            2: [some(chunk_of(-1, 0), chunk_of(1, 0))],
            5: [send_partner_chunk, project_tokens],
        },
    )
    arrive(
        3,
        0,
        {0: [some(chunk_of(0, 1))], 2: [some(chunk_of(-2, 0), chunk_of(2, 0))], 5: [right_factor]},
    )
    arrive(
        1,
        1,
        {
            0: [lambda: eliminate(0, 16)],
            1: [lambda: eliminate(16, RANK)],
            2: [some(chunk_of(-3, 0), chunk_of(3, 0))],
            3: [finish_basis],
            4: [scatter_right],
        },
    )
    arrive(4, 0, {0: [some(chunk_of(-1, 1), chunk_of(1, 1))], 2: [some(chunk_of(4, 0))]})
    arrive(2, 1, {1: [gather_tile], 5: [gather_right]})
    process(chunk_of(-2, 1), chunk_of(2, 1))
    cross_wait(1)
    cross_wait(2)
    process(chunk_of(-3, 1), chunk_of(3, 1))
    cross_wait(3)
    process(chunk_of(4, 1))
    approximate()
    err_out[0] = macc[...].astype(BF16)
    advance(0)
    for entry in pending:
        dx_hop(entry[0], 2)

    for copy in sent:
        copy.wait_send()
    for shift in range(NZ):
        for other in range(2):
            chunk = chunk_of(shift, other)

            @pl.when((chunk // 2 - y + NY) % NY != 0)
            def _():
                remote(
                    part.at[chunk], rx.at[chunk], dx_s.at[chunk], dx_r.at[chunk], at_y(1)
                ).wait_send()


def body(activations, cotangent, weight, error_buffer, warm_factor):
    dma = pltpu.SemaphoreType.DMA
    sems = [
        dma((5,)), dma((4 * PIECES,)), dma((4 * PIECES,)), dma((16 * PIECES,)), dma((16 * PIECES,)),
        dma((3,)), dma((3,)), dma((15,)), dma((15,)), dma((3,)), dma((3,)), dma((15,)), dma((15,)),
        dma((7,)), dma((7,)), dma((7,)), dma((7,)), dma((7,)), dma((7,)), dma((7,)), dma((7,)),
        dma((16,)), dma((16 * SUBS,)), dma((16 * SUBS,)),
    ]
    vmem = pltpu.VMEM
    scratch = [
        vmem((16, HIDDEN, TOK), BF16),
        vmem((WIDTH, 16 * TOK), BF16),
        vmem((WIDTH, HIDDEN), BF16),
        vmem((WIDTH, HIDDEN), BF16),
        vmem((RANK, HIDDEN), F32),
        vmem((WIDTH, HIDDEN), F32),
        vmem((WIDTH, HIDDEN), F32),
        vmem((16, WIDTH, TOK), F32),
        vmem((16, WIDTH, TOK), F32),
        vmem((16, WIDTH, TOK), F32),
        vmem((RANK, WIDTH), F32),
        vmem((16, RANK, TOK), F32),
        vmem((4, RANK, WIDTH), F32),
        vmem((8, 128), F32),
        vmem((16, RANK + 8, 128), F32),
        vmem((16, RANK + 8, 128), F32),
        vmem((NO, RANK, 256), F32),
        vmem((NO, RANK, 256), F32),
        vmem((NZ, 8, 128), F32),
        vmem((NZ, 8, 128), F32),
        vmem((NZ, 8, 128), F32),
        vmem((NO, RANK, 256), F32),
        vmem((RANK, 128), F32),
    ]
    hbm = pl.BlockSpec(memory_space=pltpu.HBM)
    vspec = pl.BlockSpec(memory_space=pltpu.VMEM)
    gradient_t, error_next, update = pl.pallas_call(
        kernel,
        out_shape=(
            jax.ShapeDtypeStruct((1, WIDTH, 2 * TOK), BF16),
            jax.ShapeDtypeStruct((1, WIDTH, HIDDEN), BF16),
            jax.ShapeDtypeStruct((ROWS, HIDDEN), BF16),
        ),
        in_specs=[hbm] * 5,
        out_specs=(vspec, vspec, vspec),
        scratch_shapes=scratch + sems,
        compiler_params=pltpu.CompilerParams(
            collective_id=0, has_side_effects=True, vmem_limit_bytes=60 * 1024 * 1024
        ),
        cost_estimate=pl.CostEstimate(flops=4600000000, bytes_accessed=8000000, transcendentals=0),
    )(
        jnp.swapaxes(activations, 1, 2), jnp.swapaxes(cotangent, 1, 2), weight, error_buffer, warm_factor.T
    )
    return jnp.swapaxes(gradient_t, 1, 2), error_next, update


def solution(mesh):
    in_specs = (
        P("dp", None, None),
        P("dp", None, "tensor"),
        P("dp", "tensor"),
        P("dp", None, "tensor"),
        P("tensor", None),
    )
    out_specs = (P("dp", "tensor", None), P("dp", None, "tensor"), P("dp", "tensor"))
    return jax.shard_map(body, mesh=mesh, in_specs=in_specs, out_specs=out_specs, check_vma=False)
```

```python
import jax
import jax.numpy as jnp
from jax import lax
from jax.experimental import pallas as pl
from jax.experimental.pallas import tpu as pltpu
from jax.sharding import PartitionSpec as P

F32 = jnp.float32
BF16 = jnp.bfloat16
MESH = pl.DeviceIdType.MESH
NZ = 8
NO = 8
NY = 8
TOK = 128
HIDDEN = 1728
WIDTH = 320
RANK = 32
ROWS = 80
PIECES = 6
PIECE = HIDDEN // PIECES
SUBS = 4
SPACING = 5
DEPTH = 4
SUB = WIDTH // SUBS
NN = (((1,), (0,)), ((), ()))
NT = (((1,), (1,)), ((), ()))
TN = (((0,), (0,)), ((), ()))


def dot(a, b, dims):
    return lax.dot_general(a, b, dims, preferred_element_type=F32)


def split3(value):
    high = value.astype(BF16)
    rest = value - high.astype(F32)
    middle = rest.astype(BF16)
    low = (rest - middle.astype(F32)).astype(BF16)
    return high, middle, low


def dot_rows(value, exact, dims):
    rows = value.shape[0]
    out = dot(jnp.concatenate(split3(value), axis=0), exact, dims)
    return out[:rows] + out[rows : 2 * rows] + out[2 * rows :]


def dot_full(a, b, dims):
    return lax.dot_general(a, b, dims, precision=lax.Precision.HIGHEST, preferred_element_type=F32)


def kernel(
    x_hbm, g_hbm, w_hbm, e_hbm, f_hbm,
    dx_out, err_out, upd_out,
    gbuf, xv, wslab, ev, fv, macc, abuf,
    part, rx, rxb, p_part,
    tbuf, pbuf, gram_own, ymsg, yall,
    sbuf, sin, s2, s2in, s3, s4, gfull,
    lsem, gx_s, gx_r, gz_s, gz_r, w_s, w_r, t_s, t_r, p_s, p_r,
    yz_s, yz_r, s1_s, s1_r, s2_s, s2_r, s3_s, s3_r, s4_s, s4_r,
    dx_s, dx_r, dxb_r,
):
    me = lax.axis_index("dp")
    y = lax.axis_index("tensor")
    z = me // NO
    slot = me % NO
    rep = me % 4
    xh = slot // 4
    own = 2 * z + xh

    def at_z(j):
        return {"dp": ((z + j + NZ) % NZ) * NO + slot, "tensor": y}

    def at_slot(j):
        return {"dp": me - slot + (slot + j) % NO, "tensor": y}

    def at_rep(j):
        return {"dp": me - rep + (rep + j) % 4, "tensor": y}

    partner = {"dp": me + 4 - 8 * xh, "tensor": y}

    def at_y(j):
        return {"dp": me, "tensor": (y + j + NY) % NY}

    def at_chunk(chunk):
        return {"dp": (chunk // 2) * NO + slot % 4 + 4 * (chunk % 2), "tensor": y}

    def remote(src, dst, send, recv, device):
        return pltpu.make_async_remote_copy(
            src_ref=src, dst_ref=dst, send_sem=send, recv_sem=recv,
            device_id=device, device_id_type=MESH,
        )

    sent = []

    def chain_send(*args):
        return send(*args)

    def send(*args):
        copy = remote(*args)
        copy.start()
        sent.append(copy)
        return copy

    my_rows = pl.ds(pl.multiple_of(rep * ROWS, 16), ROWS)
    local = [
        pltpu.make_async_copy(g_hbm.at[0], gbuf.at[own], lsem.at[0]),
        pltpu.make_async_copy(f_hbm, fv, lsem.at[1]),
        pltpu.make_async_copy(e_hbm.at[0], ev, lsem.at[2]),
        pltpu.make_async_copy(x_hbm.at[0], xv, lsem.at[3]),
        pltpu.make_async_copy(w_hbm, wslab.at[my_rows], lsem.at[4]),
    ]
    for copy in local:
        copy.start()

    barrier = pltpu.get_barrier_semaphore()
    greet = [at_chunk((own + j) % 16) for j in range(1, 16)] + [at_slot(j) for j in range(1, NO) if j != 4]
    greet += [at_y(j) for j in (-3, -2, -1, 1, 2, 3)]
    for device in greet:
        pl.semaphore_signal(barrier, inc=1, device_id=device, device_id_type=MESH)
    pl.semaphore_wait(barrier, len(greet))

    def chunk_of(shift, other):
        return 2 * ((z + shift + NZ) % NZ) + (1 - xh if other else xh)

    def pieces_of(direction, hop, other):
        if hop < NZ // 2:
            return range(PIECES)
        half = PIECES // 2
        return range(half) if direction == 0 else range(half, PIECES)

    def ring(direction, hop, other, piece):
        sign = 1 if direction == 0 else -1
        ref = gbuf.at[chunk_of(-sign * (hop - 1), other), pl.ds(piece * PIECE, PIECE)]
        k = ((direction * 4 + hop - 1) * 2 + other) * PIECES + piece
        return remote(ref, ref, gz_s.at[k], gz_r.at[k], at_z(sign))

    queues = [[], []]
    counts = [[0, 0], [0, 0]]

    def issue(direction):
        count = counts[direction]
        while queues[direction] and count[0] < count[1] + DEPTH:
            copy = ring(direction, *queues[direction].pop(0))
            copy.start()
            sent.append(copy)
            count[0] += 1

    def ring_send(direction, hop, other, piece):
        queues[direction].append((hop, other, piece))

    SHIFTS = (0, -3, 3, 4)

    def cross(k, piece):
        ref = gbuf.at[chunk_of(SHIFTS[k], 0), pl.ds(piece * PIECE, PIECE)]
        return remote(ref, ref, gx_s.at[k * PIECES + piece], gx_r.at[k * PIECES + piece], partner)

    def cross_send(k, piece):
        copy = cross(k, piece)
        copy.start()
        sent.append(copy)

    def cross_wait(k):
        for piece in range(PIECES):
            cross(k, piece).wait_recv()

    def arrive(hop, other, work):
        for step in range(len(pieces_of(0, hop, other))):
            for direction in range(2):
                piece = pieces_of(direction, hop, other)[step]
                ring(direction, hop, other, piece).wait_recv()
                counts[direction][1] += 1
                reach = 2 if other else 4
                if hop < reach and piece in pieces_of(direction, hop + 1, other):
                    ring_send(direction, hop + 1, other, piece)
                issue(direction)
                if not other and hop == 3:
                    cross_send(1 + direction, piece)
                if not other and hop == 4:
                    cross_send(3, piece)
            advance()
            for task in work.get(step, ()):
                task()

    local[0].wait()
    local[1].wait()

    factor3 = jnp.concatenate(split3(fv[...]), axis=0)

    def add3(v):
        return v[:RANK] + v[RANK : 2 * RANK] + v[2 * RANK :]

    tbuf[own] = add3(dot(factor3, gbuf[own], NN))
    tz = [
        chain_send(tbuf.at[own], tbuf.at[own], t_s.at[j - 1], t_r.at[j - 1], at_chunk((own + j) % 16))
        for j in range(1, 16)
    ]
    for piece in range(PIECES):
        ring_send(0, 1, 0, piece)
        ring_send(1, 1, 0, piece)
    issue(0)
    issue(1)
    local[4].wait()
    wcopies = [
        send(wslab.at[my_rows], wslab.at[my_rows], w_s.at[j - 1], w_r.at[j - 1], at_rep(j)) for j in range(1, 4)
    ]
    for piece in range(PIECES):
        cross_send(0, piece)
    local[2].wait()
    local[3].wait()
    macc[...] = ev[...].astype(F32)
    p_part[...] = add3(dot(factor3, ev[...], NT))

    pending = []

    def dx_hop(chunk, stage):
        turn = 1 - 2 * (chunk % 2)
        root = chunk // 2
        d = (turn * (root - y) + 2 * NY) % NY

        def near(sub, step):
            rows = pl.ds(sub * SUB, SUB)
            return remote(
                part.at[chunk, rows], rx.at[chunk, rows], dx_s.at[chunk], dx_r.at[chunk * SUBS + sub], at_y(step)
            )

        def last(sub, distance):
            rows = pl.ds(sub * SUB, SUB)
            k = chunk % 2 * NY + distance
            return remote(
                part.at[chunk, rows], rxb.at[k, rows], dx_s.at[chunk], dxb_r.at[k * SUBS + sub],
                {"dp": me, "tensor": root},
            )

        def pass_on(copy):
            for sub in range(SUBS):
                near(sub, turn).wait_recv()
                rows = pl.ds(sub * SUB, SUB)
                part[chunk, rows] += rx[chunk, rows]
                copy(sub).start()

        if stage == 0:

            @pl.when((d == 4) | (d == 5))
            def _():
                step = jnp.where(d == 4, turn, -turn)
                for sub in range(SUBS):
                    near(sub, step).start()

        elif stage == 1:

            @pl.when((d == 3) | (d == 6))
            def _():
                step = jnp.where(d == 3, turn, -turn)
                pass_on(lambda sub: near(sub, step))

        elif stage == 2:
            pl.when(d == 2)(lambda: pass_on(lambda sub: near(sub, turn)))
            pl.when(d == 7)(lambda: pass_on(lambda sub: last(sub, d)))

        elif stage == 3:
            pl.when(d == 1)(lambda: pass_on(lambda sub: last(sub, d)))

        else:

            @pl.when(d == 0)
            def _():
                lane = pl.multiple_of((chunk % 2) * TOK, TOK)
                for sub in range(SUBS):
                    rows = pl.ds(sub * SUB, SUB)
                    total = part[chunk, rows]
                    for distance in (7, 1):
                        arrived = remote(
                            part.at[chunk, rows], rxb.at[chunk % 2 * NY + distance, rows], dx_s.at[chunk],
                            dxb_r.at[(chunk % 2 * NY + distance) * SUBS + sub], at_y(1),
                        )
                        arrived.wait_recv()
                        total += rxb[chunk % 2 * NY + distance, rows]
                    dx_out[0, rows, pl.ds(lane, TOK)] = total.astype(BF16)

    clock = [0]

    def advance(spacing=SPACING):
        clock[0] += 1
        for stage in (3, 2, 1):
            for entry in pending:
                if entry[1] == stage and clock[0] - entry[2] >= spacing:
                    dx_hop(entry[0], stage)
                    entry[1:] = [stage + 1, clock[0]]

    def accumulate(chunk):
        tokens = xv[:, pl.ds(pl.multiple_of(chunk * TOK, TOK), TOK)]
        for start in range(0, HIDDEN, 512):
            stop = min(start + 512, HIDDEN)
            macc[:, start:stop] += dot(tokens, gbuf[chunk, start:stop, :], NT)

    def process(*chunks):
        for chunk in chunks:
            part[chunk] = dot(wslab[...], gbuf[chunk], NN)
            dx_hop(chunk, 0)
            pending.append([chunk, 1, clock[0]])
        for chunk in chunks:
            accumulate(chunk)

    flight = {}

    def wait_for(name):
        for copy in flight[name]:
            copy.wait_recv()

    def left_factor():
        wait_for("tz")
        t_all = jnp.concatenate([tbuf[i] for i in range(16)], axis=1)
        pbuf[rep] = p_part[...] + dot_rows(t_all, xv[...], NT)
        flight["p"] = [
            chain_send(pbuf.at[rep], pbuf.at[rep], p_s.at[j - 1], p_r.at[j - 1], at_rep(j)) for j in range(1, 4)
        ]

    def project_tokens():
        wait_for("p")
        p_t = pbuf[0] + pbuf[1] + pbuf[2] + pbuf[3]
        p_part[...] = p_t
        gram = dot_full(p_t, p_t, NT)
        for i in range(4):
            gram_own[:, RANK * i : RANK * (i + 1)] = gram[8 * i : 8 * (i + 1), :]
        packed = gram_own[...]
        y_t = dot_rows(p_t, xv[...], NN)
        for i in range(16):
            ymsg[i, :RANK] = y_t[:, TOK * i : TOK * (i + 1)]
            ymsg[i, RANK:] = packed
        yall[own] = ymsg[own]
        flight["yz"] = [
            chain_send(
                ymsg.at[(own + j) % 16], yall.at[own], yz_s.at[j - 1], yz_r.at[j - 1], at_chunk((own + j) % 16)
            )
            for j in range(1, 16)
        ]
        sbuf[6] = jnp.zeros_like(sbuf[6])
        sbuf[7] = jnp.zeros_like(sbuf[7])
        s_t = dot_rows(p_part[...], ev[...], NN)
        for i in range(7):
            width = min(256, HIDDEN - 256 * i)
            sbuf[i, :, :width] = s_t[:, 256 * i : 256 * i + width]

    def right_factor():
        wait_for("yz")
        y_sum = yall[0]
        for i in range(1, 16):
            y_sum = y_sum + yall[i]
        s_t = dot_rows(y_sum[:RANK], gbuf[own], NT)
        for i in range(7):
            width = min(256, HIDDEN - 256 * i)
            sbuf[i, :, :width] += s_t[:, 256 * i : 256 * i + width]
        sin[slot] = sbuf[slot]
        flight["s1"] = [
            chain_send(sbuf.at[(slot + j) % NO], sin.at[slot], s1_s.at[j - 1], s1_r.at[j - 1], at_slot(j))
            for j in range(1, NO)
        ]
        for i in range(4):
            gfull[8 * i : 8 * (i + 1), :RANK] = y_sum[RANK:, RANK * i : RANK * (i + 1)]

    row_id = lax.broadcasted_iota(jnp.int32, (RANK, 128), 0)
    lane_id = lax.broadcasted_iota(jnp.int32, (RANK, 128), 1)

    def eliminate(first, last):
        work = gfull[...]
        if first == 0:
            work = jnp.where(lane_id < RANK, work, jnp.where(lane_id == row_id + RANK, 1.0, 0.0))
        for j in range(first, last):
            ratio = work[:, j : j + 1] / work[j : j + 1, j : j + 1]
            ratio = jnp.where(row_id[:, :1] > j, ratio, 0.0)
            work = work - ratio * work[j : j + 1, :]
        gfull[...] = work

    def scatter_right():
        wait_for("s1")
        total = sin[0]
        for i in range(1, NO):
            total = total + sin[i]
        for i in range(NZ):
            s2[i] = total[8 * (i // 2) : 8 * (i // 2) + 8, 128 * (i % 2) : 128 * (i % 2) + 128]
        s2in[z] = s2[z]
        flight["s2"] = [
            chain_send(s2.at[(z + j) % NZ], s2in.at[z], s2_s.at[j - 1], s2_r.at[j - 1], at_z(j))
            for j in range(1, NZ)
        ]

    def gather_tile():
        wait_for("s2")
        tile = s2in[0]
        for i in range(1, NZ):
            tile = tile + s2in[i]
        s3[z] = tile
        flight["s3"] = [
            chain_send(s3.at[z], s3.at[z], s3_s.at[j - 1], s3_r.at[j - 1], at_z(j)) for j in range(1, NZ)
        ]

    def gather_right():
        wait_for("s3")
        for i in range(NZ):
            s4[slot, 8 * (i // 2) : 8 * (i // 2) + 8, 128 * (i % 2) : 128 * (i % 2) + 128] = s3[i]
        flight["s4"] = [
            chain_send(s4.at[slot], s4.at[slot], s4_s.at[j - 1], s4_r.at[j - 1], at_slot(j)) for j in range(1, NO)
        ]

    def finish_basis():
        work = gfull[...]
        pivots = jnp.sum(jnp.where(lane_id == row_id, work, 0.0), axis=1, keepdims=True)
        gfull[...] = work / jnp.sqrt(pivots)
        p_part[...] = dot_full(gfull[:, RANK : 2 * RANK], p_part[...], NN)

    def approximate():
        wait_for("s4")
        inverse = gfull[:, RANK : 2 * RANK]
        s_all = jnp.concatenate([s4[i] for i in range(7)], axis=1)[:, :HIDDEN]
        second = dot_full(inverse, s_all, NN) * 0.25
        bh, bm, bl = split3(p_part[...])
        qh, qm, ql = split3(second)
        left = jnp.concatenate([bh, bh, bm, bh, bl, bm], axis=0)
        right = jnp.concatenate([qh, qm, qh, ql, qh, qm], axis=0)
        for start in range(0, HIDDEN, 512):
            stop = min(start + 512, HIDDEN)
            block = dot(left, right[:, start:stop], TN)
            abuf[:, start:stop] = block
            macc[:, start:stop] -= block
        upd_out[...] = abuf[my_rows, :].astype(BF16)

    def some(*chunks):
        return lambda: process(*chunks)

    def weights_in():
        for copy in wcopies:
            copy.wait_recv()

    def send_partner_chunk():
        for piece in range(PIECES):
            cross(0, piece).wait_recv()
            ring_send(0, 1, 1, piece)
            ring_send(1, 1, 1, piece)
        issue(0)
        issue(1)

    flight["tz"] = tz
    arrive(1, 0, {})
    arrive(
        2,
        0,
        {
            0: [left_factor],
            1: [weights_in, some(own)],
            2: [some(chunk_of(-1, 0), chunk_of(1, 0))],
            5: [send_partner_chunk],
        },
    )
    arrive(
        3,
        0,
        {0: [some(chunk_of(0, 1))], 1: [project_tokens], 2: [some(chunk_of(-2, 0), chunk_of(2, 0))]},
    )
    arrive(
        1,
        1,
        {
            0: [some(chunk_of(-3, 0), chunk_of(3, 0))],
            2: [right_factor],
            4: [lambda: eliminate(0, 16)],
            5: [lambda: eliminate(16, RANK)],
        },
    )
    arrive(4, 0, {0: [some(chunk_of(-1, 1), chunk_of(1, 1))], 2: [some(chunk_of(4, 0))]})
    arrive(2, 1, {0: [scatter_right], 2: [finish_basis]})
    cross_wait(1)
    cross_wait(2)
    process(chunk_of(-2, 1), chunk_of(2, 1), chunk_of(-3, 1), chunk_of(3, 1))
    advance(3)
    cross_wait(3)
    process(chunk_of(4, 1))
    gather_tile()
    advance(1)
    gather_right()
    advance(0)
    approximate()
    err_out[0] = macc[...].astype(BF16)
    advance(0)
    advance(0)
    for entry in pending:
        dx_hop(entry[0], 4)

    for copy in sent:
        copy.wait_send()
    for shift in range(NZ):
        for other in range(2):
            chunk = chunk_of(shift, other)

            @pl.when((chunk // 2 - y + NY) % NY != 0)
            def _():
                remote(
                    part.at[chunk], rx.at[chunk], dx_s.at[chunk], dx_r.at[chunk], at_y(1)
                ).wait_send()


def body(activations, cotangent, weight, error_buffer, warm_factor):
    dma = pltpu.SemaphoreType.DMA
    sems = [
        dma((5,)), dma((4 * PIECES,)), dma((4 * PIECES,)), dma((16 * PIECES,)), dma((16 * PIECES,)),
        dma((3,)), dma((3,)), dma((15,)), dma((15,)), dma((3,)), dma((3,)), dma((15,)), dma((15,)),
        dma((7,)), dma((7,)), dma((7,)), dma((7,)), dma((7,)), dma((7,)), dma((7,)), dma((7,)),
        dma((16,)), dma((16 * SUBS,)), dma((16 * SUBS,)),
    ]
    vmem = pltpu.VMEM
    scratch = [
        vmem((16, HIDDEN, TOK), BF16),
        vmem((WIDTH, 16 * TOK), BF16),
        vmem((WIDTH, HIDDEN), BF16),
        vmem((WIDTH, HIDDEN), BF16),
        vmem((RANK, HIDDEN), F32),
        vmem((WIDTH, HIDDEN), F32),
        vmem((WIDTH, HIDDEN), F32),
        vmem((16, WIDTH, TOK), F32),
        vmem((16, WIDTH, TOK), F32),
        vmem((16, WIDTH, TOK), F32),
        vmem((RANK, WIDTH), F32),
        vmem((16, RANK, TOK), F32),
        vmem((4, RANK, WIDTH), F32),
        vmem((8, 128), F32),
        vmem((16, RANK + 8, 128), F32),
        vmem((16, RANK + 8, 128), F32),
        vmem((NO, RANK, 256), F32),
        vmem((NO, RANK, 256), F32),
        vmem((NZ, 8, 128), F32),
        vmem((NZ, 8, 128), F32),
        vmem((NZ, 8, 128), F32),
        vmem((NO, RANK, 256), F32),
        vmem((RANK, 128), F32),
    ]
    hbm = pl.BlockSpec(memory_space=pltpu.HBM)
    vspec = pl.BlockSpec(memory_space=pltpu.VMEM)
    gradient_t, error_next, update = pl.pallas_call(
        kernel,
        out_shape=(
            jax.ShapeDtypeStruct((1, WIDTH, 2 * TOK), BF16),
            jax.ShapeDtypeStruct((1, WIDTH, HIDDEN), BF16),
            jax.ShapeDtypeStruct((ROWS, HIDDEN), BF16),
        ),
        in_specs=[hbm] * 5,
        out_specs=(vspec, vspec, vspec),
        scratch_shapes=scratch + sems,
        compiler_params=pltpu.CompilerParams(
            collective_id=0, has_side_effects=True, vmem_limit_bytes=60 * 1024 * 1024
        ),
        cost_estimate=pl.CostEstimate(flops=4600000000, bytes_accessed=8000000, transcendentals=0),
    )(
        jnp.swapaxes(activations, 1, 2), jnp.swapaxes(cotangent, 1, 2), weight, error_buffer, warm_factor.T
    )
    return jnp.swapaxes(gradient_t, 1, 2), error_next, update


def solution(mesh):
    in_specs = (
        P("dp", None, None),
        P("dp", None, "tensor"),
        P("dp", "tensor"),
        P("dp", None, "tensor"),
        P("tensor", None),
    )
    out_specs = (P("dp", "tensor", None), P("dp", None, "tensor"), P("dp", "tensor"))
    return jax.shard_map(body, mesh=mesh, in_specs=in_specs, out_specs=out_specs, check_vma=False)
```
